32 devices in a mesh: dp: 2 (over x), expert: 16 (over z, y, core).
Axes of the slice: x: 2, y: 2, z: 4, core: 2. Of those that a mesh axis runs over, the one named last changes fastest.
Arguments:
- hidden_in: bfloat16 [2, 512, 2048], P(None, ('dp', 'expert')), may hold values from -6 to 6
- cotangent: bfloat16 [2, 512, 2048], P(None, ('dp', 'expert')), may hold values from -6 to 6
- expert_ids: int32 [2, 512, 8], P(None, ('dp', 'expert')), may hold values from 0 to 15, all different within a row; in each aligned block of 16 rows (0 to 15, 16 to 31, ..., all dimensions but the last counted through in order) at most 16 rows name the same one
- route_prob: float32 [2, 512, 8], P(None, ('dp', 'expert')), may hold values from 0.05 to 1
- swap_flags: int32 [8], replicated, may hold values 0 or 1
- gate_up: bfloat16 [16, 2048, 2, 384], P('expert', 'dp'), may hold values from -0.125 to 0.125
- down_t: bfloat16 [16, 2048, 384], P('expert', 'dp'), may hold values from -0.3125 to 0.3125
Outputs:
- hidden_out: bfloat16 [2, 512, 2048], P(None, ('dp', 'expert'))
- input_grad: bfloat16 [2, 512, 2048], P(None, ('dp', 'expert'))
- resident_gate_up: bfloat16 [16, 2048, 2, 384], P('expert', 'dp')
- resident_down: bfloat16 [16, 2048, 384], P('expert', 'dp')
The draws below stay inside these ranges and needn't reach their ends.
Inputs may be any that keep to these rules, and one draw needn't show every extreme that they name: `expert_ids`: within one microbatch the 16 tokens of one device name any one expert at most 16 times, a bound that some block reaches.
All inputs are finite; a program needn't handle non-finite values.
Results may differ from the reference program's by a relative error of at most 0.0064.
Values may be sent and summed in bfloat16 or wider, within the bound.
A program may use at most 64 MiB of HBM per device.

```python
import math
import jax
import jax.numpy as jnp
import numpy as np
from jax import lax

D = 2048
HID = 384
TOP = 8
MICRO = 2
TOK = 16
EXPERTS = 16
SRC_CAP = 16
TOKENS = 512
N_DP = 2
N_EXPERT = 16


def set_ends(entries, rng, low, high):
    place = [jax.random.randint(jax.random.fold_in(rng, axis), (), 0, length) for axis, length in enumerate(entries.shape)]
    longest = entries.shape.index(max(entries.shape))
    next_to = place[:longest] + [(place[longest] + 1) % entries.shape[longest]] + place[longest + 1:]
    return entries.at[tuple(place)].set(low).at[tuple(next_to)].set(high)


def steps_of(own_key, extent, split, low, top_value):
    gain = 1.0
    for dim, parts in split:
        heights = jax.random.uniform(jax.random.fold_in(jax.random.fold_in(own_key, 6), dim), (parts,), jnp.float32, low / len(split), top_value / len(split))
        gain = gain * jnp.repeat(jnp.exp(heights), extent[dim] // parts).reshape((-1,) + (1,) * (len(extent) - 1 - dim))
    return gain


def deal_out(key, own, number, rows, amount, top, reach, slope):
    sequence = jax.random.permutation(key, amount)
    packed, common = shares(amount, rows * top, reach, slope, True), shares(amount, rows * top, reach, slope, False)
    places = jnp.arange(amount)

    def named(tallies, rotation):
        used = int((tallies > 0).sum())
        fixed = max(1, used // 4)
        moved = fixed + (places - fixed + rotation * (used - fixed)) % max(1, amount - fixed)
        return jnp.zeros((amount,), jnp.int32).at[sequence[jnp.where(places < fixed, places, moved)]].set(jnp.asarray(tallies, jnp.int32))

    tallies = jnp.where(number % 4 == 0, named(packed, number // 4), named(common, number - number // 4 - 1))
    mixed = jax.random.permutation(jax.random.fold_in(own, 3), amount)
    source_of, sink = mixed[0:amount // 2 * 2:2], mixed[1:amount // 2 * 2:2]
    slack = jnp.minimum(tallies[source_of] - 1, reach - tallies[sink]) // 2
    slack = jnp.where((source_of == sequence[0]) | (sink == sequence[0]) | (tallies[sink] == 0), 0, jnp.maximum(slack, 0))
    moved = jax.random.randint(jax.random.fold_in(own, 4), (amount // 2,), 0, 1 << 20) % (slack + 1)
    tallies = tallies.at[source_of].add(-moved).at[sink].add(moved)
    labels = jnp.searchsorted(jnp.cumsum(tallies), jnp.arange(rows * top), side="right").astype(jnp.int32)
    listing = labels.reshape(top, rows).T
    listing = listing[jax.random.permutation(jax.random.fold_in(own, 1), rows)]
    rotation = jax.random.randint(jax.random.fold_in(own, 2), (rows, 1), 0, top)
    return jnp.take_along_axis(listing, (jnp.arange(top)[None, :] + rotation) % top, axis=1)


def shares(amount, total, most, lean, full):
    weights = [(1 << 20) // math.isqrt(rank ** lean) + 1 for rank in range(1, amount + 1)]
    largest = most if full else min(most, max(-(-total // amount), total * weights[0] // sum(weights)))
    least = 1 if total - largest >= amount - 1 else 0
    given, rest = [largest] + [least] * (amount - 1), total - largest - least * (amount - 1)
    while rest > 0:
        movable = [i for i in range(1, amount) if given[i] < largest] or [i for i in range(1, amount) if given[i] < most]
        mass, remaining = sum([weights[i] for i in movable]), rest
        for i in movable:
            addition = min(most - given[i], max(1, remaining * weights[i] // mass), rest)
            given[i] = given[i] + addition
            rest = rest - addition
    return np.array(given)


def bell_draw(own_key, shape, deviation, reach, cuts=(), held_as=jnp.bfloat16):
    factor_of = steps_of(own_key, shape, cuts, -0.22, 0.18) if cuts else 1.0
    array = jax.random.normal(own_key, shape, jnp.float32) * deviation * factor_of
    return jnp.minimum(jnp.maximum(array, -reach), reach).astype(held_as)


def setup_inputs(seed: int = 0) -> dict:
    arg_keys = jax.random.split(jax.random.key(seed), 8)
    hidden_in = bell_draw(arg_keys[0], (MICRO, TOKENS, D), 1.0, 6.0, ((1, 32),))
    cotangent = bell_draw(arg_keys[1], (MICRO, TOKENS, D), 1.0, 6.0, ((1, 32),))
    expert_ids_keys = jax.random.split(jax.random.fold_in(arg_keys[2], 1), MICRO * TOKENS // TOK)
    expert_ids_turns = jax.random.permutation(jax.random.fold_in(arg_keys[2], 3), MICRO * TOKENS // TOK)
    expert_ids = jax.vmap(lambda own, number: deal_out(jax.random.fold_in(arg_keys[2], 2), own, number, TOK, EXPERTS, TOP, SRC_CAP, 2))(expert_ids_keys, expert_ids_turns).reshape((MICRO, TOKENS, TOP))
    route_prob = jnp.clip(jnp.exp(math.log(1.0) - 2.9957323 * jax.random.uniform(arg_keys[3], (MICRO, TOKENS, TOP), jnp.float32) ** steps_of(arg_keys[3], (MICRO, TOKENS, TOP), ((1, 32),), -0.2, 0.2)), 0.05, 1.0)
    swap_flags = set_ends((jax.random.randint(arg_keys[4], (EXPERTS // 2,), 0, 2) < 1).astype(jnp.int32), jax.random.fold_in(arg_keys[4], 1), 0, 1)
    gate_up = bell_draw(arg_keys[5], (EXPERTS, D, 2, HID), D ** -0.5, 0.125, ((0, 16), (1, 2)))
    down_t = bell_draw(arg_keys[6], (EXPERTS, D, HID), HID ** -0.5, 0.3125, ((0, 16), (1, 2)))
    return {"hidden_in": hidden_in, "cotangent": cotangent, "expert_ids": expert_ids, "route_prob": route_prob, "swap_flags": swap_flags, "gate_up": gate_up, "down_t": down_t}


def expert_forward(row_block, gate_matrix, down_matrix):
    hidden_width = down_matrix.shape[1]
    projected = jnp.dot(row_block, gate_matrix, preferred_element_type=jnp.float32)
    gate_part = projected[:, :hidden_width]
    upper_part = projected[:, hidden_width:]
    hidden = (jax.nn.silu(gate_part) * upper_part).astype(jnp.bfloat16)
    output = lax.dot_general(hidden, down_matrix, (((1,), (1,)), ((), ())), preferred_element_type=jnp.float32)
    return output.astype(jnp.bfloat16), projected


def expert_backward(grad_block, projected, gate_matrix, down_matrix):
    hidden_width = down_matrix.shape[1]
    gate_part = projected[:, :hidden_width]
    upper_part = projected[:, hidden_width:]
    d_hidden = jnp.dot(grad_block, down_matrix, preferred_element_type=jnp.float32)
    sigmoid_gate = jax.nn.sigmoid(gate_part)
    d_gate = (d_hidden * upper_part * sigmoid_gate * (1.0 + gate_part * (1.0 - sigmoid_gate))).astype(jnp.bfloat16)
    d_upper = (d_hidden * gate_part * sigmoid_gate).astype(jnp.bfloat16)
    d_joined = jnp.concatenate([d_gate, d_upper], axis=1)
    d_rows = lax.dot_general(d_joined, gate_matrix, (((1,), (1,)), ((), ())), preferred_element_type=jnp.float32)
    return d_rows.astype(jnp.bfloat16)


def reference(hidden_in, cotangent, expert_ids, route_prob, swap_flags, gate_up, down_t):
    capacity = N_DP * N_EXPERT * SRC_CAP
    expert_range = jnp.arange(EXPERTS, dtype=jnp.int32)
    outputs = []
    gradients = []
    for microbatch in range(hidden_in.shape[0]):
        tokens_now = hidden_in[microbatch]
        grads_now = cotangent[microbatch]
        weights_now = route_prob[microbatch]
        flat_ids = expert_ids[microbatch].reshape(-1).astype(jnp.int32)
        sorted_rows = jnp.argsort(flat_ids, stable=True).astype(jnp.int32)
        sorted_rows = jnp.concatenate([sorted_rows, jnp.zeros((capacity,), jnp.int32)])
        counts = jnp.sum((flat_ids[None, :] == expert_range[:, None]).astype(jnp.int32), axis=1).astype(jnp.int32)
        starts = (jnp.cumsum(counts) - counts).astype(jnp.int32)
        zero_field = jnp.zeros(tokens_now.shape, jnp.float32)

        def one_expert(expert_id, carried):
            out_total, grad_total = carried
            row_index = lax.dynamic_slice(sorted_rows, (starts[expert_id].astype(jnp.int32),), (capacity,))
            valid_rows = jnp.arange(capacity, dtype=jnp.int32) < counts[expert_id]
            token_index = row_index // TOP
            top_index = row_index % TOP
            row_weight = weights_now[token_index, top_index]
            row_grads = (row_weight[:, None] * grads_now[token_index].astype(jnp.float32)).astype(jnp.bfloat16)
            gate_matrix = lax.dynamic_index_in_dim(gate_up, expert_id, 0, keepdims=False).reshape(D, 2 * HID)
            down_matrix = lax.dynamic_index_in_dim(down_t, expert_id, 0, keepdims=False)
            expert_out, projected = expert_forward(tokens_now[token_index], gate_matrix, down_matrix)
            row_input = expert_backward(row_grads, projected, gate_matrix, down_matrix)
            kept_weight = jnp.where(valid_rows, row_weight, 0.0)
            out_total = out_total.at[token_index].add(kept_weight[:, None] * expert_out.astype(jnp.float32))
            grad_total = grad_total.at[token_index].add(jnp.where(valid_rows[:, None], row_input.astype(jnp.float32), 0.0))
            return out_total, grad_total

        out_total, grad_total = lax.fori_loop(jnp.int32(0), jnp.int32(EXPERTS), one_expert, (zero_field, zero_field))
        outputs.append(out_total.astype(jnp.bfloat16))
        gradients.append(grad_total.astype(jnp.bfloat16))
    half_axis = EXPERTS // 2
    device_range = jnp.arange(EXPERTS, dtype=jnp.int32)
    flag_of = swap_flags[device_range % half_axis]
    holder = jnp.where(flag_of == 1, device_range ^ half_axis, device_range).astype(jnp.int32)
    return (jnp.stack(outputs), jnp.stack(gradients), gate_up[holder], down_t[holder])
```

```python
import functools

import jax
import jax.numpy as jnp
from jax import lax
from jax.experimental import pallas as pl
from jax.experimental.pallas import tpu as pltpu
from jax.sharding import PartitionSpec as P


def from_partner(value, axis, stride):
    mask = 2**stride
    pairs = [(source, source ^ mask) for source in range(lax.axis_size(axis))]
    return lax.ppermute(value, axis, pairs)


def expert_forward(row_block, gate_matrix, down_matrix):
    hidden_width = down_matrix.shape[1]
    projected = jnp.dot(row_block, gate_matrix, preferred_element_type=jnp.float32)
    gate_part = projected[:, :hidden_width]
    upper_part = projected[:, hidden_width:]
    hidden = (jax.nn.silu(gate_part) * upper_part).astype(jnp.bfloat16)
    output = lax.dot_general(
        hidden, down_matrix, (((1,), (1,)), ((), ())), preferred_element_type=jnp.float32
    )
    return (output.astype(jnp.bfloat16), projected)


def expert_backward(grad_block, projected, gate_matrix, down_matrix):
    hidden_width = down_matrix.shape[1]
    gate_part = projected[:, :hidden_width]
    upper_part = projected[:, hidden_width:]
    d_hidden = jnp.dot(grad_block, down_matrix, preferred_element_type=jnp.float32)
    sigmoid_gate = jax.nn.sigmoid(gate_part)
    d_gate = (
        d_hidden * upper_part * sigmoid_gate * (1.0 + gate_part * (1.0 - sigmoid_gate))
    ).astype(jnp.bfloat16)
    d_upper = (d_hidden * gate_part * sigmoid_gate).astype(jnp.bfloat16)
    d_joined = jnp.concatenate([d_gate, d_upper], axis=1)
    d_rows = lax.dot_general(
        d_joined, gate_matrix, (((1,), (1,)), ((), ())), preferred_element_type=jnp.float32
    )
    return d_rows.astype(jnp.bfloat16)


def route_matrix(ids_now, swap_flags, experts, slots, moved):
    token_count, top_count = ids_now.shape
    target = ids_now
    if moved:
        half_axis = experts // 2
        hit_mask = (ids_now % half_axis)[:, :, None] == jnp.arange(half_axis, dtype=jnp.int32)[
            None, None, :
        ]
        flipped = jnp.sum(jnp.where(hit_mask, swap_flags[None, None, :], 0), axis=2)
        target = jnp.where(flipped == 1, ids_now ^ half_axis, ids_now)
    flat_ids = target.reshape(token_count * top_count)
    one_hot = (flat_ids[:, None] == jnp.arange(experts, dtype=jnp.int32)[None, :]).astype(jnp.int32)
    earlier = jnp.cumsum(one_hot, axis=0) - one_hot
    slot_index = jnp.sum(earlier * one_hot, axis=1)
    slot_place = flat_ids * slots + slot_index
    picked = slot_place[:, None] == jnp.arange(experts * slots, dtype=jnp.int32)[None, :]
    return picked.astype(jnp.bfloat16)


def run_micro(tokens_now, grads_now, ids_now, weights_now, swap_flags, gate_full, down_full, moved):
    experts = lax.axis_size("expert")
    token_count, top_count = ids_now.shape
    model_width = tokens_now.shape[1]
    slots = 2 * token_count * top_count // experts
    picked = route_matrix(ids_now, swap_flags, experts, slots, moved)
    by_token = jnp.sum(picked.reshape(token_count, top_count, experts * slots), axis=1)
    first_axis = (((0,), (0,)), ((), ()))
    send_tokens = lax.dot_general(
        by_token, tokens_now, first_axis, preferred_element_type=jnp.float32
    )
    send_tokens = send_tokens.astype(jnp.bfloat16).reshape(experts, slots, model_width)
    row_grads = (weights_now[:, :, None] * grads_now[:, None, :].astype(jnp.float32)).astype(
        jnp.bfloat16
    )
    row_grads = row_grads.reshape(token_count * top_count, model_width)
    send_grads = lax.dot_general(picked, row_grads, first_axis, preferred_element_type=jnp.float32)
    send_grads = send_grads.astype(jnp.bfloat16).reshape(experts, slots, model_width)
    gate_matrix = gate_full.reshape(model_width, -1)
    down_matrix = down_full.reshape(model_width, -1)
    pieces = lax.all_to_all(send_tokens, "expert", split_axis=0, concat_axis=0, tiled=True)
    item_count = pieces.shape[1]
    expert_out, projected = expert_forward(
        pieces.reshape(experts * item_count, model_width), gate_matrix, down_matrix
    )
    returned = lax.all_to_all(
        expert_out.reshape(experts, item_count, model_width),
        "expert",
        split_axis=0,
        concat_axis=0,
        tiled=True,
    )
    saved = projected.reshape(experts, item_count, projected.shape[1])
    arrived = lax.all_to_all(send_grads, "expert", split_axis=0, concat_axis=0, tiled=True)
    row_input = expert_backward(
        arrived.reshape(experts * slots, model_width),
        saved.reshape(experts * slots, saved.shape[2]),
        gate_matrix,
        down_matrix,
    )
    back_grad = lax.all_to_all(
        row_input.reshape(experts, slots, model_width),
        "expert",
        split_axis=0,
        concat_axis=0,
        tiled=True,
    )
    back_rows = jnp.dot(
        picked, returned.reshape(experts * slots, model_width), preferred_element_type=jnp.float32
    )
    back_rows = back_rows.reshape(token_count, top_count, model_width)
    hidden_out = jnp.sum(weights_now[:, :, None] * back_rows, axis=1).astype(jnp.bfloat16)
    back_input = jnp.dot(
        picked, back_grad.reshape(experts * slots, model_width), preferred_element_type=jnp.float32
    )
    input_grad = jnp.sum(back_input.reshape(token_count, top_count, model_width), axis=1).astype(
        jnp.bfloat16
    )
    return (hidden_out, input_grad)


MESH = pl.DeviceIdType.MESH
LANES = 128


def dense_kernel(
    experts,
    replicas,
    hidden_ref,
    cot_ref,
    ids_ref,
    prob_ref,
    gate_hbm,
    down_hbm,
    out_ref,
    grad_ref,
    other_gate,
    other_down,
    rows,
    route,
    gate_full,
    down_full,
    send_buf,
    recv_buf,
    total,
    local_sem,
    row_send,
    row_recv,
    route_send,
    route_recv,
    sum_send,
    sum_recv,
    weight_send,
    weight_recv,
    swap_send,
    swap_recv,
):
    micro, tokens, width = hidden_ref.shape
    hid = down_hbm.shape[1]
    shard = gate_hbm.shape[0]
    stages = experts.bit_length() - 1
    half = experts // 2 * tokens
    me = lax.axis_index("expert")
    replica = lax.axis_index("dp")

    def flip(bit):
        return me + bit - 2 * bit * ((me // bit) % 2)

    partners = [(replica, flip(experts >> (s + 1))) for s in range(stages)]
    others = [(lax.rem(replica + r, replicas), me) for r in range(1, replicas)]

    own_gate = pltpu.make_async_copy(gate_hbm, gate_full.at[replica], local_sem.at[0])
    own_down = pltpu.make_async_copy(down_hbm, down_full.at[replica], local_sem.at[1])
    own_gate.start()
    own_down.start()

    barrier = pltpu.get_barrier_semaphore()
    for device in partners + others:
        pl.semaphore_signal(barrier, inc=1, device_id=device, device_id_type=MESH)

    lane = lax.broadcasted_iota(jnp.int32, (tokens, LANES), 1)
    for m in range(micro):
        rows[m, 0, 0:tokens, :] = hidden_ref[m]
        rows[m, 1, 0:tokens, :] = cot_ref[m]
        table = jnp.zeros((tokens, LANES), jnp.float32)
        for k in range(ids_ref.shape[2]):
            table = table + jnp.where(
                lane == ids_ref[m, :, k : k + 1], prob_ref[m, :, k : k + 1], 0.0
            )
        route[m, 0:tokens, :] = table

    pl.semaphore_wait(barrier, len(partners) + len(others))

    def remote(src, dst, send, recv, device):
        return pltpu.make_async_remote_copy(
            src_ref=src,
            dst_ref=dst,
            send_sem=send,
            recv_sem=recv,
            device_id=device,
            device_id_type=MESH,
        )

    def gather_stage(m, s):
        held = (1 << s) * tokens
        here, there = pl.ds(0, held), pl.ds(held, held)
        return (
            remote(
                route.at[m, here],
                route.at[m, there],
                route_send.at[m, s],
                route_recv.at[m, s],
                partners[s],
            ),
            remote(
                rows.at[m, :, here],
                rows.at[m, :, there],
                row_send.at[m, s],
                row_recv.at[m, s],
                partners[s],
            ),
        )

    def sum_stage(m, s):
        held = (1 << s) * tokens
        part = pl.ds(held, held)
        return remote(
            send_buf.at[m, :, part],
            recv_buf.at[m, :, part],
            sum_send.at[m, s],
            sum_recv.at[m, s],
            partners[s],
        )

    gathers = [[gather_stage(m, s) for s in range(stages)] for m in range(micro)]
    sums = [[sum_stage(m, s) for s in range(stages)] for m in range(micro)]
    weights = []
    for r, device in enumerate(others):
        weights.append(
            remote(
                gate_hbm,
                gate_full.at[replica],
                weight_send.at[r, 0],
                weight_recv.at[r, 0],
                device,
            )
        )
        weights.append(
            remote(
                down_hbm,
                down_full.at[replica],
                weight_send.at[r, 1],
                weight_recv.at[r, 1],
                device,
            )
        )
    swaps = [
        remote(gate_hbm, other_gate, swap_send.at[0], swap_recv.at[0], partners[0]),
        remote(down_hbm, other_down, swap_send.at[1], swap_recv.at[1], partners[0]),
    ]

    def start(copies):
        for copy in copies:
            copy.start()

    for m in range(micro):
        start(gathers[m][0])
    start(weights)
    for s in range(stages):
        for m in range(micro):
            for copy in gathers[m][s]:
                copy.wait_recv()
            if s + 1 < stages:
                start(gathers[m][s + 1])
        if s == 0:
            start(swaps)
    own_gate.wait()
    own_down.wait()
    for copy in weights:
        copy.wait_recv()

    lane_full = lax.broadcasted_iota(jnp.int32, (half, LANES), 1)
    contract_last = (((1,), (1,)), ((), ()))

    def compute(m, upper):
        first = half if upper else 0
        block = pl.ds(first, half)
        weight = jnp.sum(
            jnp.where(lane_full == me, route[m, block, :], 0.0), axis=1, keepdims=True
        )
        projected = jnp.zeros((half, 2 * hid), jnp.float32)
        d_hidden = jnp.zeros((half, hid), jnp.float32)
        for r in range(replicas):
            columns = pl.ds(r * shard, shard)
            projected = projected + jnp.dot(
                rows[m, 0, block, columns], gate_full[r], preferred_element_type=jnp.float32
            )
            row_grad = (weight * rows[m, 1, block, columns].astype(jnp.float32)).astype(
                jnp.bfloat16
            )
            d_hidden = d_hidden + jnp.dot(
                row_grad, down_full[r], preferred_element_type=jnp.float32
            )
        gate_part = projected[:, :hid]
        upper_part = projected[:, hid:]
        sigmoid_gate = jax.nn.sigmoid(gate_part)
        hidden = (gate_part * sigmoid_gate * upper_part).astype(jnp.bfloat16)
        d_gate = (
            d_hidden * upper_part * sigmoid_gate * (1.0 + gate_part * (1.0 - sigmoid_gate))
        ).astype(jnp.bfloat16)
        d_upper = (d_hidden * gate_part * sigmoid_gate).astype(jnp.bfloat16)
        d_joined = jnp.concatenate([d_gate, d_upper], axis=1)
        step = min(512, shard)
        for r in range(replicas):
            for c in range(0, shard, step):
                columns = pl.ds(r * shard + c, step)
                output = lax.dot_general(
                    hidden,
                    down_full[r, c : c + step, :],
                    contract_last,
                    preferred_element_type=jnp.float32,
                )
                output = weight * output.astype(jnp.bfloat16).astype(jnp.float32)
                row_input = lax.dot_general(
                    d_joined,
                    gate_full[r, c : c + step, :],
                    contract_last,
                    preferred_element_type=jnp.float32,
                )
                if upper:
                    send_buf[m, 0, block, columns] = output.astype(jnp.bfloat16)
                    send_buf[m, 1, block, columns] = row_input.astype(jnp.bfloat16)
                else:
                    total[m, 0, block, columns] = output
                    total[m, 1, block, columns] = row_input.astype(jnp.bfloat16).astype(
                        jnp.float32
                    )

    def reduce(m, s):
        held = (1 << s) * tokens
        sums[m][s].wait_recv()
        if s == 0:
            for i, ref in ((0, out_ref), (1, grad_ref)):
                summed = total[m, i, 0:tokens, :] + recv_buf[m, i, tokens : 2 * tokens, :].astype(
                    jnp.float32
                )
                ref[m] = summed.astype(jnp.bfloat16)
            return
        keep = held // 2
        for i in range(2):
            send_buf[m, i, keep:held, :] = (
                total[m, i, keep:held, :]
                + recv_buf[m, i, held + keep : 2 * held, :].astype(jnp.float32)
            ).astype(jnp.bfloat16)
        sums[m][s - 1].start()
        for i in range(2):
            total[m, i, 0:keep, :] = total[m, i, 0:keep, :] + recv_buf[
                m, i, held : held + keep, :
            ].astype(jnp.float32)

    last = stages - 1
    for m in range(micro):
        compute(m, True)
        sums[m][last].start()
        compute(m, False)
    for s in range(last, -1, -1):
        for m in range(micro):
            reduce(m, s)

    for m in range(micro):
        for s in range(stages):
            for copy in gathers[m][s]:
                copy.wait_send()
            sums[m][s].wait_send()
    for copy in weights:
        copy.wait_send()
    for copy in swaps:
        copy.wait()


def local_dense(hidden_in, cotangent, expert_ids, route_prob, swap_flags, gate_up, down_t):
    experts = lax.axis_size("expert")
    replicas = lax.axis_size("dp")
    half_axis = experts // 2
    my_index = lax.axis_index("expert")
    flag_mine = jnp.sum(
        jnp.where(jnp.arange(half_axis, dtype=jnp.int32) == my_index % half_axis, swap_flags, 0)
    )
    micro, tokens, width = hidden_in.shape
    shard, hid = down_t.shape[1:]
    stages = experts.bit_length() - 1
    gate = gate_up.reshape(shard, 2 * hid)
    down = down_t.reshape(shard, hid)
    all_rows = experts * tokens
    half_rows = all_rows // 2
    vmem, anywhere = pl.BlockSpec(memory_space=pltpu.VMEM), pl.BlockSpec(memory_space=pl.ANY)
    dma = pltpu.SemaphoreType.DMA
    out, grad, other_gate, other_down = pl.pallas_call(
        functools.partial(dense_kernel, experts, replicas),
        out_shape=(
            jax.ShapeDtypeStruct(hidden_in.shape, jnp.bfloat16),
            jax.ShapeDtypeStruct(hidden_in.shape, jnp.bfloat16),
            jax.ShapeDtypeStruct(gate.shape, jnp.bfloat16),
            jax.ShapeDtypeStruct(down.shape, jnp.bfloat16),
        ),
        in_specs=[vmem] * 4 + [anywhere] * 2,
        out_specs=[vmem, vmem, anywhere, anywhere],
        scratch_shapes=[
            pltpu.VMEM((micro, 2, all_rows, width), jnp.bfloat16),
            pltpu.VMEM((micro, all_rows, LANES), jnp.float32),
            pltpu.VMEM((replicas, shard, 2 * hid), jnp.bfloat16),
            pltpu.VMEM((replicas, shard, hid), jnp.bfloat16),
            pltpu.VMEM((micro, 2, all_rows, width), jnp.bfloat16),
            pltpu.VMEM((micro, 2, all_rows, width), jnp.bfloat16),
            pltpu.VMEM((micro, 2, half_rows, width), jnp.float32),
            dma((2,)),
            dma((micro, stages)),
            dma((micro, stages)),
            dma((micro, stages)),
            dma((micro, stages)),
            dma((micro, stages)),
            dma((micro, stages)),
            dma((replicas, 2)),
            dma((replicas, 2)),
            dma((2,)),
            dma((2,)),
        ],
        compiler_params=pltpu.CompilerParams(
            collective_id=0, has_side_effects=True, vmem_limit_bytes=50 * 2**20
        ),
        cost_estimate=pl.CostEstimate(
            flops=micro * all_rows * width * hid * 12,
            bytes_accessed=8 * shard * replicas * hid * 6,
            transcendentals=micro * all_rows * hid,
        ),
    )(hidden_in, cotangent, expert_ids, route_prob, gate, down)
    moved = flag_mine == 1
    return (
        out,
        grad,
        jnp.where(moved, other_gate.reshape(gate_up.shape), gate_up),
        jnp.where(moved, other_down.reshape(down_t.shape), down_t),
    )


def pick_plan(mesh):
    experts = mesh.shape["expert"]
    small = experts <= 16 and experts & (experts - 1) == 0
    return local_dense if small else local_routed


def local_routed(hidden_in, cotangent, expert_ids, route_prob, swap_flags, gate_up, down_t):
    experts = lax.axis_size("expert")
    swap_bit = experts.bit_length() - 2
    half_axis = experts // 2
    my_index = lax.axis_index("expert")
    flag_mine = jnp.sum(
        jnp.where(jnp.arange(half_axis, dtype=jnp.int32) == my_index % half_axis, swap_flags, 0)
    )
    gate_full, down_full = (
        lax.all_gather(gate_up, "dp", axis=1, tiled=True),
        lax.all_gather(down_t, "dp", axis=1, tiled=True),
    )
    out_first, grad_first = run_micro(
        hidden_in[0],
        cotangent[0],
        expert_ids[0],
        route_prob[0],
        swap_flags,
        gate_full,
        down_full,
        False,
    )
    other_gate, other_down = from_partner((gate_up, down_t), "expert", swap_bit)
    resident_gate_up = jnp.where(flag_mine == 1, other_gate, gate_up)
    resident_down = jnp.where(flag_mine == 1, other_down, down_t)
    gate_full, down_full = (
        lax.all_gather(resident_gate_up, "dp", axis=1, tiled=True),
        lax.all_gather(resident_down, "dp", axis=1, tiled=True),
    )
    out_second, grad_second = run_micro(
        hidden_in[1],
        cotangent[1],
        expert_ids[1],
        route_prob[1],
        swap_flags,
        gate_full,
        down_full,
        True,
    )
    return (
        jnp.stack([out_first, out_second]),
        jnp.stack([grad_first, grad_second]),
        resident_gate_up,
        resident_down,
    )


def solution(mesh):
    placed = (
        P(None, ("dp", "expert"), None),
        P(None, ("dp", "expert"), None),
        P(None, ("dp", "expert"), None),
        P(None, ("dp", "expert"), None),
        P(),
        P("expert", "dp", None, None),
        P("expert", "dp", None),
    )
    return jax.shard_map(
        pick_plan(mesh),
        mesh=mesh,
        in_specs=placed,
        out_specs=(
            P(None, ("dp", "expert"), None),
            P(None, ("dp", "expert"), None),
            P("expert", "dp", None, None),
            P("expert", "dp", None),
        ),
        check_vma=False,
    )
```

```python
import functools

import jax
import jax.numpy as jnp
from jax import lax
from jax.experimental import pallas as pl
from jax.experimental.pallas import tpu as pltpu
from jax.sharding import PartitionSpec as P


def from_partner(value, axis, stride):
    mask = 2**stride
    pairs = [(source, source ^ mask) for source in range(lax.axis_size(axis))]
    return lax.ppermute(value, axis, pairs)


def expert_forward(row_block, gate_matrix, down_matrix):
    hidden_width = down_matrix.shape[1]
    projected = jnp.dot(row_block, gate_matrix, preferred_element_type=jnp.float32)
    gate_part = projected[:, :hidden_width]
    upper_part = projected[:, hidden_width:]
    hidden = (jax.nn.silu(gate_part) * upper_part).astype(jnp.bfloat16)
    output = lax.dot_general(
        hidden, down_matrix, (((1,), (1,)), ((), ())), preferred_element_type=jnp.float32
    )
    return (output.astype(jnp.bfloat16), projected)


def expert_backward(grad_block, projected, gate_matrix, down_matrix):
    hidden_width = down_matrix.shape[1]
    gate_part = projected[:, :hidden_width]
    upper_part = projected[:, hidden_width:]
    d_hidden = jnp.dot(grad_block, down_matrix, preferred_element_type=jnp.float32)
    sigmoid_gate = jax.nn.sigmoid(gate_part)
    d_gate = (
        d_hidden * upper_part * sigmoid_gate * (1.0 + gate_part * (1.0 - sigmoid_gate))
    ).astype(jnp.bfloat16)
    d_upper = (d_hidden * gate_part * sigmoid_gate).astype(jnp.bfloat16)
    d_joined = jnp.concatenate([d_gate, d_upper], axis=1)
    d_rows = lax.dot_general(
        d_joined, gate_matrix, (((1,), (1,)), ((), ())), preferred_element_type=jnp.float32
    )
    return d_rows.astype(jnp.bfloat16)


def route_matrix(ids_now, swap_flags, experts, slots, moved):
    token_count, top_count = ids_now.shape
    target = ids_now
    if moved:
        half_axis = experts // 2
        hit_mask = (ids_now % half_axis)[:, :, None] == jnp.arange(half_axis, dtype=jnp.int32)[
            None, None, :
        ]
        flipped = jnp.sum(jnp.where(hit_mask, swap_flags[None, None, :], 0), axis=2)
        target = jnp.where(flipped == 1, ids_now ^ half_axis, ids_now)
    flat_ids = target.reshape(token_count * top_count)
    one_hot = (flat_ids[:, None] == jnp.arange(experts, dtype=jnp.int32)[None, :]).astype(jnp.int32)
    earlier = jnp.cumsum(one_hot, axis=0) - one_hot
    slot_index = jnp.sum(earlier * one_hot, axis=1)
    slot_place = flat_ids * slots + slot_index
    picked = slot_place[:, None] == jnp.arange(experts * slots, dtype=jnp.int32)[None, :]
    return picked.astype(jnp.bfloat16)


def run_micro(tokens_now, grads_now, ids_now, weights_now, swap_flags, gate_full, down_full, moved):
    experts = lax.axis_size("expert")
    token_count, top_count = ids_now.shape
    model_width = tokens_now.shape[1]
    slots = 2 * token_count * top_count // experts
    picked = route_matrix(ids_now, swap_flags, experts, slots, moved)
    by_token = jnp.sum(picked.reshape(token_count, top_count, experts * slots), axis=1)
    first_axis = (((0,), (0,)), ((), ()))
    send_tokens = lax.dot_general(
        by_token, tokens_now, first_axis, preferred_element_type=jnp.float32
    )
    send_tokens = send_tokens.astype(jnp.bfloat16).reshape(experts, slots, model_width)
    row_grads = (weights_now[:, :, None] * grads_now[:, None, :].astype(jnp.float32)).astype(
        jnp.bfloat16
    )
    row_grads = row_grads.reshape(token_count * top_count, model_width)
    send_grads = lax.dot_general(picked, row_grads, first_axis, preferred_element_type=jnp.float32)
    send_grads = send_grads.astype(jnp.bfloat16).reshape(experts, slots, model_width)
    gate_matrix = gate_full.reshape(model_width, -1)
    down_matrix = down_full.reshape(model_width, -1)
    pieces = lax.all_to_all(send_tokens, "expert", split_axis=0, concat_axis=0, tiled=True)
    item_count = pieces.shape[1]
    expert_out, projected = expert_forward(
        pieces.reshape(experts * item_count, model_width), gate_matrix, down_matrix
    )
    returned = lax.all_to_all(
        expert_out.reshape(experts, item_count, model_width),
        "expert",
        split_axis=0,
        concat_axis=0,
        tiled=True,
    )
    saved = projected.reshape(experts, item_count, projected.shape[1])
    arrived = lax.all_to_all(send_grads, "expert", split_axis=0, concat_axis=0, tiled=True)
    row_input = expert_backward(
        arrived.reshape(experts * slots, model_width),
        saved.reshape(experts * slots, saved.shape[2]),
        gate_matrix,
        down_matrix,
    )
    back_grad = lax.all_to_all(
        row_input.reshape(experts, slots, model_width),
        "expert",
        split_axis=0,
        concat_axis=0,
        tiled=True,
    )
    back_rows = jnp.dot(
        picked, returned.reshape(experts * slots, model_width), preferred_element_type=jnp.float32
    )
    back_rows = back_rows.reshape(token_count, top_count, model_width)
    hidden_out = jnp.sum(weights_now[:, :, None] * back_rows, axis=1).astype(jnp.bfloat16)
    back_input = jnp.dot(
        picked, back_grad.reshape(experts * slots, model_width), preferred_element_type=jnp.float32
    )
    input_grad = jnp.sum(back_input.reshape(token_count, top_count, model_width), axis=1).astype(
        jnp.bfloat16
    )
    return (hidden_out, input_grad)


MESH = pl.DeviceIdType.MESH
LANES = 128


def swap_group(pair):
    return (pair // 4) * 2 + pair % 2


def dense_kernel(
    experts,
    replicas,
    skipped,
    hidden_ref,
    cot_ref,
    ids_ref,
    prob_ref,
    gate_hbm,
    down_hbm,
    out_ref,
    grad_ref,
    other_gate,
    other_down,
    rows,
    route,
    gate_full,
    down_full,
    send_buf,
    recv_buf,
    total,
    local_sem,
    row_send,
    row_recv,
    route_send,
    route_recv,
    sum_send,
    sum_recv,
    weight_send,
    weight_recv,
    swap_send,
    swap_recv,
):
    micro, tokens, width = hidden_ref.shape
    hid = down_hbm.shape[1]
    shard = gate_hbm.shape[0]
    stages = experts.bit_length() - 1
    half = experts // 2 * tokens
    me = lax.axis_index("expert")
    replica = lax.axis_index("dp")

    def flip(bit):
        return me + bit - 2 * bit * ((me // bit) % 2)

    partners = [(replica, flip(experts >> (s + 1))) for s in range(stages)]
    others = [(lax.rem(replica + r, replicas), me) for r in range(1, replicas)]

    own_gate = pltpu.make_async_copy(gate_hbm, gate_full.at[replica], local_sem.at[0])
    own_down = pltpu.make_async_copy(down_hbm, down_full.at[replica], local_sem.at[1])
    own_gate.start()
    own_down.start()

    barrier = pltpu.get_barrier_semaphore()
    for device in partners + others:
        pl.semaphore_signal(barrier, inc=1, device_id=device, device_id_type=MESH)

    lane = lax.broadcasted_iota(jnp.int32, (tokens, LANES), 1)
    for m in range(micro):
        rows[m, 0, 0:tokens, :] = hidden_ref[m]
        rows[m, 1, 0:tokens, :] = cot_ref[m]
        table = jnp.zeros((tokens, LANES), jnp.float32)
        for k in range(ids_ref.shape[2]):
            table = table + jnp.where(
                lane == ids_ref[m, :, k : k + 1], prob_ref[m, :, k : k + 1], 0.0
            )
        route[m, 0:tokens, :] = table

    pl.semaphore_wait(barrier, len(partners) + len(others))

    def remote(src, dst, send, recv, device):
        return pltpu.make_async_remote_copy(
            src_ref=src,
            dst_ref=dst,
            send_sem=send,
            recv_sem=recv,
            device_id=device,
            device_id_type=MESH,
        )

    def gather_stage(m, s):
        held = (1 << s) * tokens
        here, there = pl.ds(0, held), pl.ds(held, held)
        return (
            remote(
                route.at[m, here],
                route.at[m, there],
                route_send.at[m, s],
                route_recv.at[m, s],
                partners[s],
            ),
            remote(
                rows.at[m, :, here],
                rows.at[m, :, there],
                row_send.at[m, s],
                row_recv.at[m, s],
                partners[s],
            ),
        )

    def sum_stage(m, s):
        held = (1 << s) * tokens
        part = pl.ds(held, held)
        return remote(
            send_buf.at[m, :, part],
            recv_buf.at[m, :, part],
            sum_send.at[m, s],
            sum_recv.at[m, s],
            partners[s],
        )

    gathers = [[gather_stage(m, s) for s in range(stages)] for m in range(micro)]
    sums = [[sum_stage(m, s) for s in range(stages)] for m in range(micro)]
    weights = []
    for r, device in enumerate(others):
        weights.append(
            remote(
                gate_hbm,
                gate_full.at[replica],
                weight_send.at[r, 0],
                weight_recv.at[r, 0],
                device,
            )
        )
        weights.append(
            remote(
                down_hbm,
                down_full.at[replica],
                weight_send.at[r, 1],
                weight_recv.at[r, 1],
                device,
            )
        )
    swaps = [
        remote(gate_hbm, other_gate, swap_send.at[0], swap_recv.at[0], partners[0]),
        remote(down_hbm, other_down, swap_send.at[1], swap_recv.at[1], partners[0]),
    ]

    def start(copies):
        for copy in copies:
            copy.start()

    def if_swapped(action):
        if skipped is None:
            action()
        else:
            pl.when(swap_group(me % (experts // 2)) != skipped)(action)

    for m in range(micro):
        start(gathers[m][0])
    start(weights)
    for s in range(stages):
        for m in range(micro):
            for copy in gathers[m][s]:
                copy.wait_recv()
            if s + 1 < stages:
                start(gathers[m][s + 1])
        if s == 0:
            if_swapped(lambda: start(swaps))
    own_gate.wait()
    own_down.wait()
    for copy in weights:
        copy.wait_recv()

    lane_full = lax.broadcasted_iota(jnp.int32, (half, LANES), 1)
    contract_last = (((1,), (1,)), ((), ()))

    def compute(m, upper):
        first = half if upper else 0
        block = pl.ds(first, half)
        weight = jnp.sum(
            jnp.where(lane_full == me, route[m, block, :], 0.0), axis=1, keepdims=True
        )
        projected = jnp.zeros((half, 2 * hid), jnp.float32)
        d_hidden = jnp.zeros((half, hid), jnp.float32)
        for r in range(replicas):
            columns = pl.ds(r * shard, shard)
            projected = projected + jnp.dot(
                rows[m, 0, block, columns], gate_full[r], preferred_element_type=jnp.float32
            )
            row_grad = (weight * rows[m, 1, block, columns].astype(jnp.float32)).astype(
                jnp.bfloat16
            )
            d_hidden = d_hidden + jnp.dot(
                row_grad, down_full[r], preferred_element_type=jnp.float32
            )
        gate_part = projected[:, :hid]
        upper_part = projected[:, hid:]
        sigmoid_gate = jax.nn.sigmoid(gate_part)
        hidden = (gate_part * sigmoid_gate * upper_part).astype(jnp.bfloat16)
        d_gate = (
            d_hidden * upper_part * sigmoid_gate * (1.0 + gate_part * (1.0 - sigmoid_gate))
        ).astype(jnp.bfloat16)
        d_upper = (d_hidden * gate_part * sigmoid_gate).astype(jnp.bfloat16)
        d_joined = jnp.concatenate([d_gate, d_upper], axis=1)
        step = min(512, shard)
        for r in range(replicas):
            for c in range(0, shard, step):
                columns = pl.ds(r * shard + c, step)
                output = lax.dot_general(
                    hidden,
                    down_full[r, c : c + step, :],
                    contract_last,
                    preferred_element_type=jnp.float32,
                )
                output = weight * output.astype(jnp.bfloat16).astype(jnp.float32)
                row_input = lax.dot_general(
                    d_joined,
                    gate_full[r, c : c + step, :],
                    contract_last,
                    preferred_element_type=jnp.float32,
                )
                if upper:
                    send_buf[m, 0, block, columns] = output.astype(jnp.bfloat16)
                    send_buf[m, 1, block, columns] = row_input.astype(jnp.bfloat16)
                else:
                    total[m, 0, block, columns] = output
                    total[m, 1, block, columns] = row_input.astype(jnp.bfloat16).astype(
                        jnp.float32
                    )

    def reduce(m, s):
        held = (1 << s) * tokens
        sums[m][s].wait_recv()
        if s == 0:
            for i, ref in ((0, out_ref), (1, grad_ref)):
                summed = total[m, i, 0:tokens, :] + recv_buf[m, i, tokens : 2 * tokens, :].astype(
                    jnp.float32
                )
                ref[m] = summed.astype(jnp.bfloat16)
            return
        keep = held // 2
        for i in range(2):
            send_buf[m, i, keep:held, :] = (
                total[m, i, keep:held, :]
                + recv_buf[m, i, held + keep : 2 * held, :].astype(jnp.float32)
            ).astype(jnp.bfloat16)
        sums[m][s - 1].start()
        for i in range(2):
            total[m, i, 0:keep, :] = total[m, i, 0:keep, :] + recv_buf[
                m, i, held : held + keep, :
            ].astype(jnp.float32)

    last = stages - 1
    for m in range(micro):
        compute(m, True)
        sums[m][last].start()
        compute(m, False)
    for s in range(last, -1, -1):
        for m in range(micro):
            reduce(m, s)

    for m in range(micro):
        for s in range(stages):
            for copy in gathers[m][s]:
                copy.wait_send()
            sums[m][s].wait_send()
    for copy in weights:
        copy.wait_send()

    def finish_swaps():
        for copy in swaps:
            copy.wait()

    if_swapped(finish_swaps)


def local_dense(hidden_in, cotangent, expert_ids, route_prob, swap_flags, gate_up, down_t):
    experts = lax.axis_size("expert")
    replicas = lax.axis_size("dp")
    half_axis = experts // 2
    my_index = lax.axis_index("expert")
    flag_mine = jnp.sum(
        jnp.where(jnp.arange(half_axis, dtype=jnp.int32) == my_index % half_axis, swap_flags, 0)
    )
    micro, tokens, width = hidden_in.shape
    shard, hid = down_t.shape[1:]
    stages = experts.bit_length() - 1
    gate = gate_up.reshape(shard, 2 * hid)
    down = down_t.reshape(shard, hid)
    all_rows = experts * tokens
    half_rows = all_rows // 2
    vmem, anywhere = pl.BlockSpec(memory_space=pltpu.VMEM), pl.BlockSpec(memory_space=pl.ANY)
    dma = pltpu.SemaphoreType.DMA
    def run(skipped, *operands):
        return pl.pallas_call(
            functools.partial(dense_kernel, experts, replicas, skipped),
            out_shape=(
                jax.ShapeDtypeStruct(hidden_in.shape, jnp.bfloat16),
                jax.ShapeDtypeStruct(hidden_in.shape, jnp.bfloat16),
                jax.ShapeDtypeStruct(gate.shape, jnp.bfloat16),
                jax.ShapeDtypeStruct(down.shape, jnp.bfloat16),
            ),
            in_specs=[vmem] * 4 + [anywhere] * 2,
            out_specs=[vmem, vmem, anywhere, anywhere],
            scratch_shapes=[
                pltpu.VMEM((micro, 2, all_rows, width), jnp.bfloat16),
                pltpu.VMEM((micro, all_rows, LANES), jnp.float32),
                pltpu.VMEM((replicas, shard, 2 * hid), jnp.bfloat16),
                pltpu.VMEM((replicas, shard, hid), jnp.bfloat16),
                pltpu.VMEM((micro, 2, all_rows, width), jnp.bfloat16),
                pltpu.VMEM((micro, 2, all_rows, width), jnp.bfloat16),
                pltpu.VMEM((micro, 2, half_rows, width), jnp.float32),
                dma((2,)),
                dma((micro, stages)),
                dma((micro, stages)),
                dma((micro, stages)),
                dma((micro, stages)),
                dma((micro, stages)),
                dma((micro, stages)),
                dma((replicas, 2)),
                dma((replicas, 2)),
                dma((2,)),
                dma((2,)),
            ],
            compiler_params=pltpu.CompilerParams(
                collective_id=0 if skipped is None else 1 + skipped, has_side_effects=True, vmem_limit_bytes=50 * 2**20
            ),
            cost_estimate=pl.CostEstimate(
                flops=micro * all_rows * width * hid * 12,
                bytes_accessed=8 * shard * replicas * hid * 6,
                transcendentals=micro * all_rows * hid,
            ),
        )(*operands)

    groups = (half_axis + 3) // 4 * 2
    pair_group = swap_group(jnp.arange(half_axis, dtype=jnp.int32))
    in_group = pair_group[None, :] == jnp.arange(groups, dtype=jnp.int32)[:, None]
    active = jnp.max(jnp.where(in_group, swap_flags[None, :], 0), axis=1)
    idle = jnp.where(active == 0, jnp.arange(1, groups + 1, dtype=jnp.int32), 0)
    out, grad, other_gate, other_down = lax.switch(
        jnp.max(idle),
        [functools.partial(run, skipped) for skipped in (None, *range(groups))],
        hidden_in,
        cotangent,
        expert_ids,
        route_prob,
        gate,
        down,
    )
    moved = flag_mine == 1
    return (
        out,
        grad,
        jnp.where(moved, other_gate.reshape(gate_up.shape), gate_up),
        jnp.where(moved, other_down.reshape(down_t.shape), down_t),
    )


def pick_plan(mesh):
    experts = mesh.shape["expert"]
    small = experts <= 16 and experts & (experts - 1) == 0
    return local_dense if small else local_routed


def local_routed(hidden_in, cotangent, expert_ids, route_prob, swap_flags, gate_up, down_t):
    experts = lax.axis_size("expert")
    swap_bit = experts.bit_length() - 2
    half_axis = experts // 2
    my_index = lax.axis_index("expert")
    flag_mine = jnp.sum(
        jnp.where(jnp.arange(half_axis, dtype=jnp.int32) == my_index % half_axis, swap_flags, 0)
    )
    gate_full, down_full = (
        lax.all_gather(gate_up, "dp", axis=1, tiled=True),
        lax.all_gather(down_t, "dp", axis=1, tiled=True),
    )
    out_first, grad_first = run_micro(
        hidden_in[0],
        cotangent[0],
        expert_ids[0],
        route_prob[0],
        swap_flags,
        gate_full,
        down_full,
        False,
    )
    other_gate, other_down = from_partner((gate_up, down_t), "expert", swap_bit)
    resident_gate_up = jnp.where(flag_mine == 1, other_gate, gate_up)
    resident_down = jnp.where(flag_mine == 1, other_down, down_t)
    gate_full, down_full = (
        lax.all_gather(resident_gate_up, "dp", axis=1, tiled=True),
        lax.all_gather(resident_down, "dp", axis=1, tiled=True),
    )
    out_second, grad_second = run_micro(
        hidden_in[1],
        cotangent[1],
        expert_ids[1],
        route_prob[1],
        swap_flags,
        gate_full,
        down_full,
        True,
    )
    return (
        jnp.stack([out_first, out_second]),
        jnp.stack([grad_first, grad_second]),
        resident_gate_up,
        resident_down,
    )


def solution(mesh):
    placed = (
        P(None, ("dp", "expert"), None),
        P(None, ("dp", "expert"), None),
        P(None, ("dp", "expert"), None),
        P(None, ("dp", "expert"), None),
        P(),
        P("expert", "dp", None, None),
        P("expert", "dp", None),
    )
    return jax.shard_map(
        pick_plan(mesh),
        mesh=mesh,
        in_specs=placed,
        out_specs=(
            P(None, ("dp", "expert"), None),
            P(None, ("dp", "expert"), None),
            P("expert", "dp", None, None),
            P("expert", "dp", None),
        ),
        check_vma=False,
    )
```

```python
import functools

import jax
import jax.numpy as jnp
from jax import lax
from jax.experimental import pallas as pl
from jax.experimental.pallas import tpu as pltpu
from jax.sharding import PartitionSpec as P


def from_partner(value, axis, stride):
    mask = 2**stride
    pairs = [(source, source ^ mask) for source in range(lax.axis_size(axis))]
    return lax.ppermute(value, axis, pairs)


def expert_forward(row_block, gate_matrix, down_matrix):
    hidden_width = down_matrix.shape[1]
    projected = jnp.dot(row_block, gate_matrix, preferred_element_type=jnp.float32)
    gate_part = projected[:, :hidden_width]
    upper_part = projected[:, hidden_width:]
    hidden = (jax.nn.silu(gate_part) * upper_part).astype(jnp.bfloat16)
    output = lax.dot_general(
        hidden, down_matrix, (((1,), (1,)), ((), ())), preferred_element_type=jnp.float32
    )
    return (output.astype(jnp.bfloat16), projected)


def expert_backward(grad_block, projected, gate_matrix, down_matrix):
    hidden_width = down_matrix.shape[1]
    gate_part = projected[:, :hidden_width]
    upper_part = projected[:, hidden_width:]
    d_hidden = jnp.dot(grad_block, down_matrix, preferred_element_type=jnp.float32)
    sigmoid_gate = jax.nn.sigmoid(gate_part)
    d_gate = (
        d_hidden * upper_part * sigmoid_gate * (1.0 + gate_part * (1.0 - sigmoid_gate))
    ).astype(jnp.bfloat16)
    d_upper = (d_hidden * gate_part * sigmoid_gate).astype(jnp.bfloat16)
    d_joined = jnp.concatenate([d_gate, d_upper], axis=1)
    d_rows = lax.dot_general(
        d_joined, gate_matrix, (((1,), (1,)), ((), ())), preferred_element_type=jnp.float32
    )
    return d_rows.astype(jnp.bfloat16)


def route_matrix(ids_now, swap_flags, experts, slots, moved):
    token_count, top_count = ids_now.shape
    target = ids_now
    if moved:
        half_axis = experts // 2
        hit_mask = (ids_now % half_axis)[:, :, None] == jnp.arange(half_axis, dtype=jnp.int32)[
            None, None, :
        ]
        flipped = jnp.sum(jnp.where(hit_mask, swap_flags[None, None, :], 0), axis=2)
        target = jnp.where(flipped == 1, ids_now ^ half_axis, ids_now)
    flat_ids = target.reshape(token_count * top_count)
    one_hot = (flat_ids[:, None] == jnp.arange(experts, dtype=jnp.int32)[None, :]).astype(jnp.int32)
    earlier = jnp.cumsum(one_hot, axis=0) - one_hot
    slot_index = jnp.sum(earlier * one_hot, axis=1)
    slot_place = flat_ids * slots + slot_index
    picked = slot_place[:, None] == jnp.arange(experts * slots, dtype=jnp.int32)[None, :]
    return picked.astype(jnp.bfloat16)


def run_micro(tokens_now, grads_now, ids_now, weights_now, swap_flags, gate_full, down_full, moved):
    experts = lax.axis_size("expert")
    token_count, top_count = ids_now.shape
    model_width = tokens_now.shape[1]
    slots = 2 * token_count * top_count // experts
    picked = route_matrix(ids_now, swap_flags, experts, slots, moved)
    by_token = jnp.sum(picked.reshape(token_count, top_count, experts * slots), axis=1)
    first_axis = (((0,), (0,)), ((), ()))
    send_tokens = lax.dot_general(
        by_token, tokens_now, first_axis, preferred_element_type=jnp.float32
    )
    send_tokens = send_tokens.astype(jnp.bfloat16).reshape(experts, slots, model_width)
    row_grads = (weights_now[:, :, None] * grads_now[:, None, :].astype(jnp.float32)).astype(
        jnp.bfloat16
    )
    row_grads = row_grads.reshape(token_count * top_count, model_width)
    send_grads = lax.dot_general(picked, row_grads, first_axis, preferred_element_type=jnp.float32)
    send_grads = send_grads.astype(jnp.bfloat16).reshape(experts, slots, model_width)
    gate_matrix = gate_full.reshape(model_width, -1)
    down_matrix = down_full.reshape(model_width, -1)
    pieces = lax.all_to_all(send_tokens, "expert", split_axis=0, concat_axis=0, tiled=True)
    item_count = pieces.shape[1]
    expert_out, projected = expert_forward(
        pieces.reshape(experts * item_count, model_width), gate_matrix, down_matrix
    )
    returned = lax.all_to_all(
        expert_out.reshape(experts, item_count, model_width),
        "expert",
        split_axis=0,
        concat_axis=0,
        tiled=True,
    )
    saved = projected.reshape(experts, item_count, projected.shape[1])
    arrived = lax.all_to_all(send_grads, "expert", split_axis=0, concat_axis=0, tiled=True)
    row_input = expert_backward(
        arrived.reshape(experts * slots, model_width),
        saved.reshape(experts * slots, saved.shape[2]),
        gate_matrix,
        down_matrix,
    )
    back_grad = lax.all_to_all(
        row_input.reshape(experts, slots, model_width),
        "expert",
        split_axis=0,
        concat_axis=0,
        tiled=True,
    )
    back_rows = jnp.dot(
        picked, returned.reshape(experts * slots, model_width), preferred_element_type=jnp.float32
    )
    back_rows = back_rows.reshape(token_count, top_count, model_width)
    hidden_out = jnp.sum(weights_now[:, :, None] * back_rows, axis=1).astype(jnp.bfloat16)
    back_input = jnp.dot(
        picked, back_grad.reshape(experts * slots, model_width), preferred_element_type=jnp.float32
    )
    input_grad = jnp.sum(back_input.reshape(token_count, top_count, model_width), axis=1).astype(
        jnp.bfloat16
    )
    return (hidden_out, input_grad)


MESH = pl.DeviceIdType.MESH
LANES = 128


def swap_group(pair):
    return (pair // 4) * 2 + pair % 2


def dense_kernel(
    experts,
    replicas,
    skipped,
    hidden_ref,
    cot_ref,
    ids_ref,
    prob_ref,
    gate_hbm,
    down_hbm,
    out_ref,
    grad_ref,
    other_gate,
    other_down,
    rows,
    route,
    gate_full,
    down_full,
    send_buf,
    recv_buf,
    total,
    local_sem,
    row_send,
    row_recv,
    route_send,
    route_recv,
    sum_send,
    sum_recv,
    weight_send,
    weight_recv,
    swap_send,
    swap_recv,
):
    micro, tokens, width = hidden_ref.shape
    hid = down_hbm.shape[1]
    shard = gate_hbm.shape[0]
    stages = experts.bit_length() - 1
    half = experts // 2 * tokens
    me = lax.axis_index("expert")
    replica = lax.axis_index("dp")

    def flip(bit):
        return me + bit - 2 * bit * ((me // bit) % 2)

    partners = [(replica, flip(experts >> (s + 1))) for s in range(stages)]
    others = [(lax.rem(replica + r, replicas), me) for r in range(1, replicas)]

    own_gate = pltpu.make_async_copy(gate_hbm, gate_full.at[replica], local_sem.at[0])
    own_down = pltpu.make_async_copy(down_hbm, down_full.at[replica], local_sem.at[1])
    own_gate.start()
    own_down.start()

    barrier = pltpu.get_barrier_semaphore()
    for device in partners + others:
        pl.semaphore_signal(barrier, inc=1, device_id=device, device_id_type=MESH)

    lane = lax.broadcasted_iota(jnp.int32, (tokens, LANES), 1)
    for m in range(micro):
        rows[m, 0, 0:tokens, :] = hidden_ref[m]
        rows[m, 1, 0:tokens, :] = cot_ref[m]
        table = jnp.zeros((tokens, LANES), jnp.float32)
        for k in range(ids_ref.shape[2]):
            table = table + jnp.where(
                lane == ids_ref[m, :, k : k + 1], prob_ref[m, :, k : k + 1], 0.0
            )
        route[m, 0:tokens, :] = table

    pl.semaphore_wait(barrier, len(partners) + len(others))

    def remote(src, dst, send, recv, device):
        return pltpu.make_async_remote_copy(
            src_ref=src,
            dst_ref=dst,
            send_sem=send,
            recv_sem=recv,
            device_id=device,
            device_id_type=MESH,
        )

    def gather_stage(m, s):
        held = (1 << s) * tokens
        here, there = pl.ds(0, held), pl.ds(held, held)
        return (
            remote(
                route.at[m, here],
                route.at[m, there],
                route_send.at[m, s],
                route_recv.at[m, s],
                partners[s],
            ),
            remote(
                rows.at[m, :, here],
                rows.at[m, :, there],
                row_send.at[m, s],
                row_recv.at[m, s],
                partners[s],
            ),
        )

    def sum_stage(m, s):
        held = (1 << s) * tokens
        part = pl.ds(held, held)
        return remote(
            send_buf.at[m, :, part],
            recv_buf.at[m, :, part],
            sum_send.at[m, s],
            sum_recv.at[m, s],
            partners[s],
        )

    gathers = [[gather_stage(m, s) for s in range(stages)] for m in range(micro)]
    sums = [[sum_stage(m, s) for s in range(stages)] for m in range(micro)]
    weights = []
    for r, device in enumerate(others):
        weights.append(
            remote(
                gate_hbm,
                gate_full.at[replica],
                weight_send.at[r, 0],
                weight_recv.at[r, 0],
                device,
            )
        )
        weights.append(
            remote(
                down_hbm,
                down_full.at[replica],
                weight_send.at[r, 1],
                weight_recv.at[r, 1],
                device,
            )
        )
    swaps = [
        remote(gate_hbm, other_gate, swap_send.at[0], swap_recv.at[0], partners[0]),
        remote(down_hbm, other_down, swap_send.at[1], swap_recv.at[1], partners[0]),
    ]

    def start(copies):
        for copy in copies:
            copy.start()

    def if_swapped(action):
        if skipped is None:
            action()
        else:
            pl.when(swap_group(me % (experts // 2)) != skipped)(action)

    for m in range(micro):
        start(gathers[m][0])
    start(weights)
    for s in range(stages):
        for m in range(micro):
            for copy in gathers[m][s]:
                copy.wait_recv()
            if s + 1 < stages:
                start(gathers[m][s + 1])
        if s == 0:
            if_swapped(lambda: start(swaps))
    own_gate.wait()
    own_down.wait()
    for copy in weights:
        copy.wait_recv()

    lane_full = lax.broadcasted_iota(jnp.int32, (half, LANES), 1)
    contract_last = (((1,), (1,)), ((), ()))

    def compute(m, upper):
        first = half if upper else 0
        block = pl.ds(first, half)
        weight = jnp.sum(
            jnp.where(lane_full == me, route[m, block, :], 0.0), axis=1, keepdims=True
        )
        projected = jnp.zeros((half, 2 * hid), jnp.float32)
        d_hidden = jnp.zeros((half, hid), jnp.float32)
        for r in range(replicas):
            columns = pl.ds(r * shard, shard)
            projected = projected + jnp.dot(
                rows[m, 0, block, columns], gate_full[r], preferred_element_type=jnp.float32
            )
            row_grad = (weight * rows[m, 1, block, columns].astype(jnp.float32)).astype(
                jnp.bfloat16
            )
            d_hidden = d_hidden + jnp.dot(
                row_grad, down_full[r], preferred_element_type=jnp.float32
            )
        gate_part = projected[:, :hid]
        upper_part = projected[:, hid:]
        sigmoid_gate = jax.nn.sigmoid(gate_part)
        hidden = (gate_part * sigmoid_gate * upper_part).astype(jnp.bfloat16)
        d_gate = (
            d_hidden * upper_part * sigmoid_gate * (1.0 + gate_part * (1.0 - sigmoid_gate))
        ).astype(jnp.bfloat16)
        d_upper = (d_hidden * gate_part * sigmoid_gate).astype(jnp.bfloat16)
        d_joined = jnp.concatenate([d_gate, d_upper], axis=1)
        step = min(512, shard)
        for r in range(replicas):
            for c in range(0, shard, step):
                columns = pl.ds(r * shard + c, step)
                output = lax.dot_general(
                    hidden,
                    down_full[r, c : c + step, :],
                    contract_last,
                    preferred_element_type=jnp.float32,
                )
                output = weight * output.astype(jnp.bfloat16).astype(jnp.float32)
                row_input = lax.dot_general(
                    d_joined,
                    gate_full[r, c : c + step, :],
                    contract_last,
                    preferred_element_type=jnp.float32,
                )
                if upper:
                    send_buf[m, 0, block, columns] = output.astype(jnp.bfloat16)
                    send_buf[m, 1, block, columns] = row_input.astype(jnp.bfloat16)
                else:
                    total[m, 0, block, columns] = output
                    total[m, 1, block, columns] = row_input.astype(jnp.bfloat16).astype(
                        jnp.float32
                    )

    def reduce(m, s):
        held = (1 << s) * tokens
        sum_stage(m, s).wait_recv()
        if s == 0:
            for i, ref in ((0, out_ref), (1, grad_ref)):
                summed = total[m, i, 0:tokens, :] + recv_buf[m, i, tokens : 2 * tokens, :].astype(
                    jnp.float32
                )
                ref[m] = summed.astype(jnp.bfloat16)
            return
        keep = held // 2
        for i in range(2):
            send_buf[m, i, keep:held, :] = (
                total[m, i, keep:held, :]
                + recv_buf[m, i, held + keep : 2 * held, :].astype(jnp.float32)
            ).astype(jnp.bfloat16)
        sum_stage(m, s - 1).start()
        for i in range(2):
            total[m, i, 0:keep, :] = total[m, i, 0:keep, :] + recv_buf[
                m, i, held : held + keep, :
            ].astype(jnp.float32)

    last = stages - 1

    def expert_step(m, carry):
        compute(m, True)
        sum_stage(m, last).start()
        compute(m, False)
        return carry

    lax.fori_loop(0, micro, expert_step, 0)
    for s in range(last, -1, -1):

        def reduce_step(m, carry, s=s):
            reduce(m, s)
            return carry

        lax.fori_loop(0, micro, reduce_step, 0)

    for m in range(micro):
        for s in range(stages):
            for copy in gathers[m][s]:
                copy.wait_send()
            sums[m][s].wait_send()
    for copy in weights:
        copy.wait_send()

    def finish_swaps():
        for copy in swaps:
            copy.wait()

    if_swapped(finish_swaps)


def local_dense(hidden_in, cotangent, expert_ids, route_prob, swap_flags, gate_up, down_t):
    experts = lax.axis_size("expert")
    replicas = lax.axis_size("dp")
    half_axis = experts // 2
    my_index = lax.axis_index("expert")
    flag_mine = jnp.sum(
        jnp.where(jnp.arange(half_axis, dtype=jnp.int32) == my_index % half_axis, swap_flags, 0)
    )
    micro, tokens, width = hidden_in.shape
    shard, hid = down_t.shape[1:]
    stages = experts.bit_length() - 1
    gate = gate_up.reshape(shard, 2 * hid)
    down = down_t.reshape(shard, hid)
    all_rows = experts * tokens
    half_rows = all_rows // 2
    vmem, anywhere = pl.BlockSpec(memory_space=pltpu.VMEM), pl.BlockSpec(memory_space=pl.ANY)
    dma = pltpu.SemaphoreType.DMA
    def run(skipped, *operands):
        return pl.pallas_call(
            functools.partial(dense_kernel, experts, replicas, skipped),
            out_shape=(
                jax.ShapeDtypeStruct(hidden_in.shape, jnp.bfloat16),
                jax.ShapeDtypeStruct(hidden_in.shape, jnp.bfloat16),
                jax.ShapeDtypeStruct(gate.shape, jnp.bfloat16),
                jax.ShapeDtypeStruct(down.shape, jnp.bfloat16),
            ),
            in_specs=[vmem] * 4 + [anywhere] * 2,
            out_specs=[vmem, vmem, anywhere, anywhere],
            scratch_shapes=[
                pltpu.VMEM((micro, 2, all_rows, width), jnp.bfloat16),
                pltpu.VMEM((micro, all_rows, LANES), jnp.float32),
                pltpu.VMEM((replicas, shard, 2 * hid), jnp.bfloat16),
                pltpu.VMEM((replicas, shard, hid), jnp.bfloat16),
                pltpu.VMEM((micro, 2, all_rows, width), jnp.bfloat16),
                pltpu.VMEM((micro, 2, all_rows, width), jnp.bfloat16),
                pltpu.VMEM((micro, 2, half_rows, width), jnp.float32),
                dma((2,)),
                dma((micro, stages)),
                dma((micro, stages)),
                dma((micro, stages)),
                dma((micro, stages)),
                dma((micro, stages)),
                dma((micro, stages)),
                dma((replicas, 2)),
                dma((replicas, 2)),
                dma((2,)),
                dma((2,)),
            ],
            compiler_params=pltpu.CompilerParams(
                collective_id=0 if skipped is None else 1 + skipped, has_side_effects=True, vmem_limit_bytes=50 * 2**20
            ),
            cost_estimate=pl.CostEstimate(
                flops=micro * all_rows * width * hid * 12,
                bytes_accessed=8 * shard * replicas * hid * 6,
                transcendentals=micro * all_rows * hid,
            ),
        )(*operands)

    groups = (half_axis + 3) // 4 * 2
    pair_group = swap_group(jnp.arange(half_axis, dtype=jnp.int32))
    in_group = pair_group[None, :] == jnp.arange(groups, dtype=jnp.int32)[:, None]
    active = jnp.max(jnp.where(in_group, swap_flags[None, :], 0), axis=1)
    idle = jnp.where(active == 0, jnp.arange(1, groups + 1, dtype=jnp.int32), 0)
    out, grad, other_gate, other_down = lax.switch(
        jnp.max(idle),
        [functools.partial(run, skipped) for skipped in (None, *range(groups))],
        hidden_in,
        cotangent,
        expert_ids,
        route_prob,
        gate,
        down,
    )
    moved = flag_mine == 1
    return (
        out,
        grad,
        jnp.where(moved, other_gate.reshape(gate_up.shape), gate_up),
        jnp.where(moved, other_down.reshape(down_t.shape), down_t),
    )


def pick_plan(mesh):
    experts = mesh.shape["expert"]
    small = experts <= 16 and experts & (experts - 1) == 0
    return local_dense if small else local_routed


def local_routed(hidden_in, cotangent, expert_ids, route_prob, swap_flags, gate_up, down_t):
    experts = lax.axis_size("expert")
    swap_bit = experts.bit_length() - 2
    half_axis = experts // 2
    my_index = lax.axis_index("expert")
    flag_mine = jnp.sum(
        jnp.where(jnp.arange(half_axis, dtype=jnp.int32) == my_index % half_axis, swap_flags, 0)
    )
    gate_full, down_full = (
        lax.all_gather(gate_up, "dp", axis=1, tiled=True),
        lax.all_gather(down_t, "dp", axis=1, tiled=True),
    )
    out_first, grad_first = run_micro(
        hidden_in[0],
        cotangent[0],
        expert_ids[0],
        route_prob[0],
        swap_flags,
        gate_full,
        down_full,
        False,
    )
    other_gate, other_down = from_partner((gate_up, down_t), "expert", swap_bit)
    resident_gate_up = jnp.where(flag_mine == 1, other_gate, gate_up)
    resident_down = jnp.where(flag_mine == 1, other_down, down_t)
    gate_full, down_full = (
        lax.all_gather(resident_gate_up, "dp", axis=1, tiled=True),
        lax.all_gather(resident_down, "dp", axis=1, tiled=True),
    )
    out_second, grad_second = run_micro(
        hidden_in[1],
        cotangent[1],
        expert_ids[1],
        route_prob[1],
        swap_flags,
        gate_full,
        down_full,
        True,
    )
    return (
        jnp.stack([out_first, out_second]),
        jnp.stack([grad_first, grad_second]),
        resident_gate_up,
        resident_down,
    )


def solution(mesh):
    placed = (
        P(None, ("dp", "expert"), None),
        P(None, ("dp", "expert"), None),
        P(None, ("dp", "expert"), None),
        P(None, ("dp", "expert"), None),
        P(),
        P("expert", "dp", None, None),
        P("expert", "dp", None),
    )
    return jax.shard_map(
        pick_plan(mesh),
        mesh=mesh,
        in_specs=placed,
        out_specs=(
            P(None, ("dp", "expert"), None),
            P(None, ("dp", "expert"), None),
            P("expert", "dp", None, None),
            P("expert", "dp", None),
        ),
        check_vma=False,
    )
```
